512 devices in a mesh: replica: 64 (over x, z_lo, y), fsdp: 8 (over z_hi, core).
Axes of the slice: x: 4, y: 8, z: 8 (z_hi: 4, z_lo: 2; z = z_hi * 2 + z_lo), core: 2. Of those that a mesh axis runs over, the one named last changes fastest.
Arguments:
- tokens: bfloat16 [64, 1024, 8192], P('replica', 'fsdp'), may hold values from -6 to 6
- norm_gain: bfloat16 [64, 8192], P('replica'), may hold values from 0.25 to 1.75
- key_weight: bfloat16 [64, 8192, 512], P('replica', 'fsdp'), may hold values from -0.0625 to 0.0625
- key_target: bfloat16 [64, 1024, 512], P('replica', 'fsdp'), may hold values from -6 to 6
- outer_base: float32 [64, 8192], P('fsdp'), may hold values from -6 to 6
- outer_momentum: float32 [64, 8192], P('fsdp'), may hold values from -4 to 4
- replica_params: bfloat16 [64, 64, 8192], P('replica', 'fsdp'), may hold values from -6 to 6
Outputs:
- key_grad: bfloat16 [64, 8192, 512], P('replica', 'fsdp')
- base_next: float32 [64, 8192], P('fsdp')
- momentum_next: float32 [64, 8192], P('fsdp')
- params_next: bfloat16 [64, 64, 8192], P('replica', 'fsdp')
The draws below stay inside these ranges and needn't reach their ends.
All inputs are finite; a program needn't handle non-finite values.
Results may differ from the reference program's by a relative error of at most 0.015.
Values may be sent and summed in bfloat16 or wider, within the bound.
No kernel may reach another device: no remote copies, remote signals or barrier semaphores. Data moves between devices by JAX's collectives and lax.ppermute only.
A program may use at most 64 MiB of HBM per device.

```python
import math
import jax
import jax.numpy as jnp
from jax import lax

D = 8192
KV = 512
BLOCK = 128
TOKENS = 1024
SLAB = 64
N_REPLICA = 64


def block_levels(rng, shape, pieces, low, largest):
    loudness, own = 1.0, jax.random.fold_in(rng, 6)
    for dim, blocks in pieces:
        draws = jnp.exp(jax.random.uniform(jax.random.fold_in(own, dim), (blocks,), jnp.float32, low / len(pieces), largest / len(pieces)))
        loudness = loudness * jnp.repeat(draws, shape[dim] // blocks).reshape([-1 if axis == dim else 1 for axis in range(len(shape))])
    return loudness


def noise(own_key, dims, scale, most, pieces=(), dtype=jnp.bfloat16):
    level = block_levels(own_key, dims, pieces, -0.22, 0.18) if pieces else 1.0
    array = jax.random.normal(own_key, dims, jnp.float32) * scale * level
    return jnp.minimum(jnp.maximum(array, -most), most).astype(dtype)


def setup_inputs(seed: int = 0) -> dict:
    streams_of = jax.random.split(jax.random.key(seed), 8)
    return {
        "tokens": noise(streams_of[0], (N_REPLICA, TOKENS, D), 1.0, 6.0, ((0, 64), (1, 8))),
        "norm_gain": jnp.clip(1.0 + 0.15 * jax.random.normal(streams_of[1], (N_REPLICA, D), jnp.float32), 0.25, 1.75).astype(jnp.bfloat16),
        "key_weight": noise(streams_of[2], (N_REPLICA, D, KV), D ** -0.5, 0.0625, ((0, 64), (1, 8))),
        "key_target": noise(streams_of[3], (N_REPLICA, TOKENS, KV), 1.0, 6.0, ((0, 64), (1, 8))),
        "outer_base": noise(streams_of[4], (SLAB, D), 1.0, 6.0, ((0, 8),), jnp.float32),
        "outer_momentum": noise(streams_of[5], (SLAB, D), 0.5, 4.0, ((0, 8),), jnp.float32),
        "replica_params": noise(streams_of[6], (N_REPLICA, SLAB, D), 1.0, 6.0, ((0, 64), (1, 8))),
    }


def inner_step(operands):
    hidden, gain, weight, target = operands
    values = hidden.astype(jnp.float32)
    scaled = lax.rsqrt(lax.optimization_barrier(jnp.mean(values * values, axis=-1, keepdims=True)) + 1e-05)
    normed = (values * scaled * gain.astype(jnp.float32)[None, :]).astype(jnp.bfloat16)
    keys = jnp.dot(normed, weight, preferred_element_type=jnp.float32)
    key_cot = ((keys - target.astype(jnp.float32)) * (1.0 / math.sqrt(TOKENS))).astype(jnp.bfloat16)
    grad = lax.dot_general(normed, key_cot, (((0,), (0,)), ((), ())), preferred_element_type=jnp.float32)
    return grad.astype(jnp.bfloat16)

def reference(tokens, norm_gain, key_weight, key_target, outer_base, outer_momentum, replica_params):
    key_grad = lax.map(inner_step, (tokens, norm_gain, key_weight, key_target))
    delta = outer_base[None, :, :] - replica_params.astype(jnp.float32)
    blocks = delta.reshape(N_REPLICA, -1, BLOCK)
    block_scale = (lax.optimization_barrier(jnp.max(jnp.abs(blocks), axis=-1)) + 1e-06).astype(jnp.bfloat16)
    wide_scale = block_scale.astype(jnp.float32)[:, :, None]
    quant = (blocks * (448.0 / wide_scale)).astype(jnp.bfloat16)
    restored = quant.astype(jnp.float32) * (wide_scale / 448.0)
    mean_delta = lax.optimization_barrier(jnp.sum(restored, axis=0)) / N_REPLICA
    momentum_flat = outer_momentum.reshape(-1, BLOCK)
    base_flat = outer_base.reshape(-1, BLOCK)
    momentum_next = 0.9 * momentum_flat + mean_delta
    base_next = base_flat - 0.7 * (mean_delta + 0.9 * momentum_next)
    base_next = base_next.reshape(SLAB, D)
    momentum_next = momentum_next.reshape(SLAB, D)
    params_next = (0.5 * replica_params.astype(jnp.float32) + 0.5 * base_next[None, :, :]).astype(jnp.bfloat16)
    return (key_grad, base_next, momentum_next, params_next)
```

```python
import math

import jax
import jax.numpy as jnp
from jax import lax
from jax.sharding import PartitionSpec as P

XMODE = "a"
OUTER = "ag4"
BAR = 1
BACK = "a"
SPREAD = "g"
CHIPS = 4
CORES = 2
SAME = [[CORES * z + c for z in range(CHIPS)] for c in range(CORES)]
SWAP = [(i, i ^ 1) for i in range(CHIPS * CORES)]
ORDER = (2, 1, 3)
F32 = jnp.float32
BF16 = jnp.bfloat16


def mesh_groups(replicas):
    plane = [[r for r in range(replicas) if (r // 8) % 2 == z] for z in range(2)]
    pairs = [(r, r ^ 8) for r in range(replicas)]
    return plane, pairs


def hop(x, dz):
    pairs = [
        (CORES * z + c, CORES * ((z + dz) % CHIPS) + c) for z in range(CHIPS) for c in range(CORES)
    ]
    return lax.ppermute(x, "fsdp", pairs)


def chips_all_to_all(x):
    return lax.all_to_all(
        x, "fsdp", split_axis=0, concat_axis=0, axis_index_groups=SAME, tiled=True
    )


def stage_groups(replicas):
    parts = [[], [], []]
    for r in range(replicas):
        x, z, y = r // 16, (r // 8) % 2, r % 8
        keys = ((z, y), (x, z, y // 4), (x, y % 4))
        for part, key in zip(parts, keys):
            part.append((key, r))
    out = []
    for part in parts:
        names = sorted({key for key, _ in part})
        out.append([[r for key, r in part if key == name] for name in names])
    return out


def reduce_by_fours(x):
    for groups in stage_groups(lax.axis_size("replica")):
        got = lax.all_gather(x, "replica", axis=0, axis_index_groups=groups)
        total = jnp.sum(got.astype(F32), axis=0)
        x = total.astype(BF16)
    return total


def outer(outer_base, outer_momentum, params):
    rows, width = outer_base.shape
    replicas = lax.axis_size("replica")
    plane, pairs = mesh_groups(replicas)
    delta = outer_base - params.astype(F32)
    blocks = delta.reshape(rows, width // 128, 128)
    scale = (jnp.max(jnp.abs(blocks), axis=-1, keepdims=True) + 1e-06).astype(BF16).astype(F32)
    quant = (blocks * (448.0 / scale)).astype(BF16)
    restored = (quant.astype(F32) * (scale / 448.0)).astype(BF16)
    if OUTER == "ag4":
        total = reduce_by_fours(restored.reshape(-1, 128)).reshape(rows, width)
        return finish(outer_base, outer_momentum, params, total / replicas)
    members = len(plane[0])
    pieces = restored.reshape(members, rows * width // 128 // members, 128)
    got = lax.all_to_all(
        pieces, "replica", split_axis=0, concat_axis=0, axis_index_groups=plane, tiled=True
    )
    part = jnp.sum(got.astype(F32), axis=0)
    total = part + lax.ppermute(part, "replica", pairs)
    mean = (total / replicas).astype(BF16)
    spread = jnp.broadcast_to(mean[None], pieces.shape)
    mean_delta = lax.all_to_all(
        spread, "replica", split_axis=0, concat_axis=0, axis_index_groups=plane, tiled=True
    )
    return finish(outer_base, outer_momentum, params, mean_delta.reshape(rows, width).astype(F32))


def finish(outer_base, outer_momentum, params, mean_delta):
    momentum_next = 0.9 * outer_momentum + mean_delta
    base_next = outer_base - 0.7 * (mean_delta + 0.9 * momentum_next)
    params_next = (0.5 * params.astype(F32) + 0.5 * base_next).astype(BF16)
    return base_next, momentum_next, params_next


def shards(tokens, norm_gain, key_weight, key_target, outer_base, outer_momentum, replica_params):
    tok = tokens[0]
    rows, width = tok.shape
    weights = key_weight[0]
    depth, cols = weights.shape
    me = lax.axis_index("fsdp")
    core = me % CORES
    chip = me // CORES
    wide = CORES * depth
    root = 1.0 / math.sqrt(rows * CHIPS * CORES)
    dims = (((0,), (0,)), ((), ()))

    if XMODE == "a":
        x = chips_all_to_all(tok.reshape(rows, CHIPS, wide).transpose(1, 0, 2))
    else:
        got = {}
        for dz in (0,) + ORDER:
            piece = lax.dynamic_slice(tok, (0, (chip + dz) % CHIPS * wide), (rows, wide))
            got[dz] = hop(piece, dz) if dz else piece
        x = jnp.stack([got[dz] for dz in range(CHIPS)], axis=0)

    gain = lax.dynamic_slice(norm_gain[0], (me * depth,), (depth,)).astype(F32)[:, None]
    mine = (weights.astype(F32) * gain).astype(BF16)
    other = lax.ppermute(mine, "fsdp", SWAP)
    chip_weights = jnp.where(
        core == 0, jnp.concatenate([mine, other], 0), jnp.concatenate([other, mine], 0)
    )
    values = tok.astype(F32)
    inv = lax.rsqrt(jnp.mean(values * values, axis=-1, keepdims=True) + 1e-05)

    if BAR == 3:
        x, outer_base = lax.optimization_barrier((x, outer_base))
    base_next, momentum_next, params_next = outer(outer_base, outer_momentum, replica_params[0])
    if BAR == 1:
        x, base_next, momentum_next, params_next = lax.optimization_barrier((x, base_next, momentum_next, params_next))

    x = x.reshape(CHIPS * rows, wide)
    x_mine = lax.dynamic_slice(x, (0, core * depth), (CHIPS * rows, depth))
    x_send = lax.dynamic_slice(x, (0, (1 - core) * depth), (CHIPS * rows, depth))
    x_other = lax.ppermute(x_send, "fsdp", SWAP)
    part = jnp.dot(x, chip_weights, preferred_element_type=F32).astype(BF16).reshape(CHIPS, rows, cols)
    if XMODE == "p":
        order = (chip - jnp.arange(CHIPS)) % CHIPS
        part = jnp.take(part, order, axis=0)
    keys = jnp.sum(chips_all_to_all(part).astype(F32), axis=0)
    target = key_target[0].astype(F32)
    cot = ((keys * inv - target) * root * inv).astype(BF16)
    if SPREAD == "a":
        cots = chips_all_to_all(jnp.broadcast_to(cot[None], (CHIPS, rows, cols)))
    else:
        cots = lax.all_gather(cot, "fsdp", axis=0, axis_index_groups=SAME)
    if XMODE == "p":
        cots = jnp.take(cots, order, axis=0)
    cots = cots.reshape(CHIPS * rows, cols)
    cots_other = lax.ppermute(cots, "fsdp", SWAP)
    one = lax.dot_general(x_mine, cots, dims, preferred_element_type=F32)
    two = lax.dot_general(x_other, cots_other, dims, preferred_element_type=F32)
    key_grad = ((one + two) * gain).astype(BF16)[None]
    return (key_grad, base_next, momentum_next, params_next[None])


def solution(mesh):
    return jax.shard_map(
        shards,
        mesh=mesh,
        in_specs=(
            P("replica", "fsdp", None),
            P("replica", None),
            P("replica", "fsdp", None),
            P("replica", "fsdp", None),
            P("fsdp", None),
            P("fsdp", None),
            P("replica", "fsdp", None),
        ),
        out_specs=(
            P("replica", "fsdp", None),
            P("fsdp", None),
            P("fsdp", None),
            P("replica", "fsdp", None),
        ),
        check_vma=False,
    )
```

```python
import math

import jax
import jax.numpy as jnp
from jax import lax
from jax.experimental import pallas as pl
from jax.experimental.pallas import tpu as pltpu
from jax.sharding import PartitionSpec as P

CHIPS = 4
CORES = 2
SAME = [[CORES * z + c for z in range(CHIPS)] for c in range(CORES)]
SWAP = [(i, i ^ 1) for i in range(CHIPS * CORES)]
F32 = jnp.float32
BF16 = jnp.bfloat16
LIMIT = 40 << 20


def chips_all_to_all(x):
    return lax.all_to_all(
        x, "fsdp", split_axis=0, concat_axis=0, axis_index_groups=SAME, tiled=True
    )


def split_kernel(tok, out, held, come, go):
    wide = out.shape[2]
    ins = [
        pltpu.make_async_copy(tok.at[:, pl.ds(z * wide, wide)], held.at[z], come.at[z])
        for z in range(CHIPS)
    ]
    outs = [pltpu.make_async_copy(held.at[z], out.at[z], go.at[z]) for z in range(CHIPS)]
    for copy in ins:
        copy.start()
    for copy, after in zip(ins, outs):
        copy.wait()
        after.start()
    for after in outs:
        after.wait()


def split_features(tok):
    rows, width = tok.shape
    shape = (CHIPS, rows, width // CHIPS)
    return pl.pallas_call(
        split_kernel,
        out_shape=jax.ShapeDtypeStruct(shape, tok.dtype),
        in_specs=[pl.BlockSpec(memory_space=pl.ANY)],
        out_specs=pl.BlockSpec(memory_space=pl.ANY),
        scratch_shapes=[
            pltpu.VMEM(shape, tok.dtype),
            pltpu.SemaphoreType.DMA((CHIPS,)),
            pltpu.SemaphoreType.DMA((CHIPS,)),
        ],
        cost_estimate=pl.CostEstimate(flops=0, bytes_accessed=4 * rows * width, transcendentals=0),
    )(tok)


def keys_kernel(core, x, mine, other, out):
    chips, rows, wide = x.shape
    depth, cols = mine.shape
    near = x[:, :, pl.ds(pl.multiple_of(core[0] * depth, depth), depth)]
    far = x[:, :, pl.ds(pl.multiple_of((1 - core[0]) * depth, depth), depth)]
    near = near.reshape(chips * rows, depth)
    far = far.reshape(chips * rows, depth)
    for at in range(0, cols, 256):
        part = pl.ds(at, 256)
        total = jnp.dot(near, mine[:, part], preferred_element_type=F32)
        total = total + jnp.dot(far, other[:, part], preferred_element_type=F32)
        out[:, :, part] = total.astype(out.dtype).reshape(chips, rows, 256)


def partial_keys(core, x, mine, other):
    chips, rows, wide = x.shape
    cols = mine.shape[1]
    vmem = pl.BlockSpec(memory_space=pltpu.VMEM)
    return pl.pallas_call(
        keys_kernel,
        in_specs=[pl.BlockSpec(memory_space=pltpu.SMEM), vmem, vmem, vmem],
        out_specs=vmem,
        out_shape=jax.ShapeDtypeStruct((chips, rows, cols), BF16),
        compiler_params=pltpu.CompilerParams(vmem_limit_bytes=24 << 20),
        cost_estimate=pl.CostEstimate(
            flops=2 * chips * rows * wide * cols,
            bytes_accessed=2 * (chips * rows * (wide + cols) + wide * cols),
            transcendentals=0,
        ),
    )(core, x, mine, other)


def quantize_kernel(base, params, out):
    for k in range(base.shape[1] // 128):
        at = pl.ds(k * 128, 128)
        delta = base[:, at] - params[:, at].astype(F32)
        scale = (jnp.max(jnp.abs(delta), axis=-1, keepdims=True) + 1e-06).astype(BF16).astype(F32)
        quant = (delta * (448.0 / scale)).astype(BF16)
        out[:, at] = (quant.astype(F32) * (scale / 448.0)).astype(BF16)


def quantize(base, params):
    return pl.pallas_call(
        quantize_kernel,
        out_shape=jax.ShapeDtypeStruct(base.shape, BF16),
        cost_estimate=pl.CostEstimate(
            flops=8 * base.size, bytes_accessed=8 * base.size, transcendentals=0
        ),
    )(base, params)


def fours_along_x(replicas):
    return [[r for r in range(replicas) if r % 16 == k] for k in range(16)]


def fours_along_y(replicas):
    return [[4 * b + j for j in range(4)] for b in range(replicas // 4)]


def sum_of_sixteen(x):
    replicas = lax.axis_size("replica")
    for groups in (fours_along_x(replicas), fours_along_y(replicas)):
        got = lax.all_gather(x.astype(BF16), "replica", axis=0, axis_index_groups=groups)
        x = jnp.sum(got.astype(F32), axis=0)
    return x


def add_neighbour(x, bit):
    pairs = [(r, r ^ bit) for r in range(lax.axis_size("replica"))]
    return x + lax.ppermute(x.astype(BF16), "replica", pairs).astype(F32)


def shards(tokens, norm_gain, key_weight, key_target, outer_base, outer_momentum, replica_params):
    tok = tokens[0]
    rows, width = tok.shape
    weights = key_weight[0]
    depth, cols = weights.shape
    me = lax.axis_index("fsdp")
    core = me % CORES
    this_core = core[None].astype(jnp.int32)
    wide = CORES * depth
    root = 1.0 / math.sqrt(rows * CHIPS * CORES)
    dims = (((0,), (0,)), ((), ()))

    x = chips_all_to_all(split_features(tok))

    gain = lax.dynamic_slice(norm_gain[0], (me * depth,), (depth,)).astype(F32)[:, None]
    mine = (weights.astype(F32) * gain).astype(BF16)
    other = lax.ppermute(mine, "fsdp", SWAP)
    values = tok.astype(F32)
    inv = lax.rsqrt(jnp.mean(values * values, axis=-1, keepdims=True) + 1e-05)

    slope = root * inv
    offset = key_target[0].astype(F32) * slope
    slope = slope * inv
    summed = sum_of_sixteen(add_neighbour(quantize(outer_base, replica_params[0]), 4))

    x, summed, slope, offset = lax.optimization_barrier((x, summed, slope, offset))

    part = partial_keys(this_core, x, mine, other)
    parts = chips_all_to_all(part)
    x = x.reshape(CHIPS * rows, wide)
    x_mine = lax.dynamic_slice(x, (0, core * depth), (CHIPS * rows, depth))
    x_send = lax.dynamic_slice(x, (0, (1 - core) * depth), (CHIPS * rows, depth))
    x_other = lax.ppermute(x_send, "fsdp", SWAP)

    mean_delta = add_neighbour(summed, 8) / lax.axis_size("replica")
    momentum_next = 0.9 * outer_momentum + mean_delta
    base_next = outer_base - 0.7 * (mean_delta + 0.9 * momentum_next)
    params_next = (0.5 * replica_params.astype(F32) + 0.5 * base_next[None]).astype(BF16)

    keys = jnp.sum(parts.astype(F32), axis=0)
    cot = (keys * slope - offset).astype(BF16)
    cots = lax.all_gather(cot, "fsdp", axis=0, axis_index_groups=SAME)
    cots = cots.reshape(CHIPS * rows, cols)
    cots_other = lax.ppermute(cots, "fsdp", SWAP)
    one = lax.dot_general(x_mine, cots, dims, preferred_element_type=F32)
    two = lax.dot_general(x_other, cots_other, dims, preferred_element_type=F32)
    key_grad = ((one + two) * gain).astype(BF16)[None]
    return (key_grad, base_next, momentum_next, params_next)


def solution(mesh):
    return jax.shard_map(
        shards,
        mesh=mesh,
        in_specs=(
            P("replica", "fsdp", None),
            P("replica", None),
            P("replica", "fsdp", None),
            P("replica", "fsdp", None),
            P("fsdp", None),
            P("fsdp", None),
            P("replica", "fsdp", None),
        ),
        out_specs=(
            P("replica", "fsdp", None),
            P("fsdp", None),
            P("fsdp", None),
            P("replica", "fsdp", None),
        ),
        check_vma=False,
    )
```

```python
import math

import jax
import jax.numpy as jnp
from jax import lax
from jax.experimental import pallas as pl
from jax.experimental.pallas import tpu as pltpu
from jax.sharding import PartitionSpec as P

CHIPS = 4
CORES = 2
SAME = [[CORES * z + c for z in range(CHIPS)] for c in range(CORES)]
SWAP = [(i, i ^ 1) for i in range(CHIPS * CORES)]
F32 = jnp.float32
BF16 = jnp.bfloat16
GRAD_TILES = 4


def chips_all_to_all(x):
    return lax.all_to_all(
        x, "fsdp", split_axis=0, concat_axis=0, axis_index_groups=SAME, tiled=True
    )


def split_kernel(tok, out, held, come, go):
    wide = out.shape[2]
    ins = [
        pltpu.make_async_copy(tok.at[:, pl.ds(z * wide, wide)], held.at[z], come.at[z])
        for z in range(CHIPS)
    ]
    outs = [pltpu.make_async_copy(held.at[z], out.at[z], go.at[z]) for z in range(CHIPS)]
    for copy in ins:
        copy.start()
    for copy, after in zip(ins, outs):
        copy.wait()
        after.start()
    for after in outs:
        after.wait()


def split_features(tok):
    rows, width = tok.shape
    shape = (CHIPS, rows, width // CHIPS)
    return pl.pallas_call(
        split_kernel,
        out_shape=jax.ShapeDtypeStruct(shape, tok.dtype),
        in_specs=[pl.BlockSpec(memory_space=pl.ANY)],
        out_specs=pl.BlockSpec(memory_space=pl.ANY),
        scratch_shapes=[
            pltpu.VMEM(shape, tok.dtype),
            pltpu.SemaphoreType.DMA((CHIPS,)),
            pltpu.SemaphoreType.DMA((CHIPS,)),
        ],
        cost_estimate=pl.CostEstimate(flops=0, bytes_accessed=4 * rows * width, transcendentals=0),
    )(tok)


def keys_kernel(place, x, mine, other, offset, out):
    chips, rows, wide = x.shape
    depth, cols = mine.shape
    near = x[:, :, pl.ds(pl.multiple_of(place[0] * depth, depth), depth)]
    far = x[:, :, pl.ds(pl.multiple_of((1 - place[0]) * depth, depth), depth)]
    near = near.reshape(chips * rows, depth)
    far = far.reshape(chips * rows, depth)
    for at in range(0, cols, 256):
        part = pl.ds(at, 256)
        total = jnp.dot(near, mine[:, part], preferred_element_type=F32)
        total = total + jnp.dot(far, other[:, part], preferred_element_type=F32)
        for z in range(chips):
            own = (place[1] == z).astype(F32)
            out[z, :, part] = (total[z * rows:(z + 1) * rows] - own * offset[:, part]).astype(out.dtype)


def partial_keys(place, x, mine, other, offset):
    chips, rows, wide = x.shape
    cols = mine.shape[1]
    vmem = pl.BlockSpec(memory_space=pltpu.VMEM)
    return pl.pallas_call(
        keys_kernel,
        in_specs=[pl.BlockSpec(memory_space=pltpu.SMEM), vmem, vmem, vmem, vmem],
        out_specs=vmem,
        out_shape=jax.ShapeDtypeStruct((chips, rows, cols), BF16),
        compiler_params=pltpu.CompilerParams(vmem_limit_bytes=16 << 20),
        cost_estimate=pl.CostEstimate(
            flops=2 * chips * rows * wide * cols,
            bytes_accessed=2 * (chips * rows * (wide + cols) + wide * cols),
            transcendentals=0,
        ),
    )(place, x, mine, other, offset)


def quantize_kernel(base, params, out):
    for k in range(base.shape[1] // 128):
        at = pl.ds(k * 128, 128)
        delta = base[:, at] - params[:, at].astype(F32)
        scale = (jnp.max(jnp.abs(delta), axis=-1, keepdims=True) + 1e-06).astype(BF16).astype(F32)
        quant = (delta * (448.0 / scale)).astype(BF16)
        out[:, at] = (quant.astype(F32) * (scale / 448.0)).astype(BF16)


def quantize(base, params):
    return pl.pallas_call(
        quantize_kernel,
        out_shape=jax.ShapeDtypeStruct(base.shape, BF16),
        cost_estimate=pl.CostEstimate(
            flops=8 * base.size, bytes_accessed=8 * base.size, transcendentals=0
        ),
    )(base, params)


def gradient_kernel(x, a, first, gain, out, held, go):
    depth = x.shape[1]
    tile = depth // GRAD_TILES
    copies = []
    for k in range(GRAD_TILES):
        part = pl.ds(k * tile, tile)
        total = first[part] + lax.dot_general(
            x[:, part], a[...], (((0,), (0,)), ((), ())), preferred_element_type=F32
        )
        held[part] = (total * gain[part]).astype(held.dtype)
        copy = pltpu.make_async_copy(held.at[part], out.at[part], go.at[k])
        copy.start()
        copies.append(copy)
    for copy in copies:
        copy.wait()


def gradient(x, a, first, gain):
    rows, depth = x.shape
    cols = a.shape[1]
    vmem = pl.BlockSpec(memory_space=pltpu.VMEM)
    return pl.pallas_call(
        gradient_kernel,
        in_specs=[vmem] * 4,
        out_specs=pl.BlockSpec(memory_space=pl.ANY),
        out_shape=jax.ShapeDtypeStruct((depth, cols), BF16),
        scratch_shapes=[pltpu.VMEM((depth, cols), BF16), pltpu.SemaphoreType.DMA((GRAD_TILES,))],
        compiler_params=pltpu.CompilerParams(vmem_limit_bytes=16 << 20),
        cost_estimate=pl.CostEstimate(
            flops=2 * rows * depth * cols,
            bytes_accessed=2 * rows * (depth + cols) + 6 * depth * cols,
            transcendentals=0,
        ),
    )(x, a, first, gain)


def fours_along_x(replicas):
    return [[r for r in range(replicas) if r % 16 == k] for k in range(16)]


def fours_along_y(replicas):
    return [[4 * b + j for j in range(4)] for b in range(replicas // 4)]


def sum_of_sixteen(x):
    replicas = lax.axis_size("replica")
    for groups in (fours_along_x(replicas), fours_along_y(replicas)):
        got = lax.all_gather(x.astype(BF16), "replica", axis=0, axis_index_groups=groups)
        x = jnp.sum(got.astype(F32), axis=0)
    return x


def add_neighbour(x, bit):
    pairs = [(r, r ^ bit) for r in range(lax.axis_size("replica"))]
    return x + lax.ppermute(x.astype(BF16), "replica", pairs).astype(F32)


def shards(tokens, norm_gain, key_weight, key_target, outer_base, outer_momentum, replica_params):
    tok = tokens[0]
    rows, width = tok.shape
    weights = key_weight[0]
    depth, cols = weights.shape
    me = lax.axis_index("fsdp")
    core = me % CORES
    place = jnp.stack([core, me // CORES]).astype(jnp.int32)
    wide = CORES * depth
    root = 1.0 / math.sqrt(rows * CHIPS * CORES)
    dims = (((0,), (0,)), ((), ()))

    pieces, outer_base, norm_gain = lax.optimization_barrier(
        (split_features(tok), outer_base, norm_gain)
    )
    x = chips_all_to_all(pieces)

    gain = lax.dynamic_slice(norm_gain[0], (me * depth,), (depth,)).astype(F32)[:, None]
    mine = (weights.astype(F32) * gain).astype(BF16)
    other = lax.ppermute(mine, "fsdp", SWAP)
    values = tok.astype(F32)
    inv = lax.rsqrt(jnp.mean(values * values, axis=-1, keepdims=True) + 1e-05)

    offset = key_target[0].astype(F32) / inv
    slope = root * inv * inv
    summed = sum_of_sixteen(add_neighbour(quantize(outer_base, replica_params[0]), 4))

    x, summed, slope, offset = lax.optimization_barrier((x, summed, slope, offset))

    part = partial_keys(place, x, mine, other, offset)
    parts = chips_all_to_all(part)
    x = x.reshape(CHIPS * rows, wide)
    x_mine = lax.dynamic_slice(x, (0, core * depth), (CHIPS * rows, depth))
    x_send = lax.dynamic_slice(x, (0, (1 - core) * depth), (CHIPS * rows, depth))
    x_other = lax.ppermute(x_send, "fsdp", SWAP)

    mean_delta = add_neighbour(summed, 8) / lax.axis_size("replica")
    momentum_next = 0.9 * outer_momentum + mean_delta
    base_next = outer_base - 0.7 * (mean_delta + 0.9 * momentum_next)
    params_next = (0.5 * replica_params.astype(F32) + 0.5 * base_next[None]).astype(BF16)

    keys = jnp.sum(parts.astype(F32), axis=0)
    cot = (keys * slope).astype(BF16)
    cots = lax.all_gather(cot, "fsdp", axis=0, axis_index_groups=SAME)
    cots = cots.reshape(CHIPS * rows, cols)
    cots_other = lax.ppermute(cots, "fsdp", SWAP)
    one = lax.dot_general(x_mine, cots, dims, preferred_element_type=F32)
    key_grad = gradient(x_other, cots_other, one, gain)[None]
    return (key_grad, base_next, momentum_next, params_next)


def solution(mesh):
    return jax.shard_map(
        shards,
        mesh=mesh,
        in_specs=(
            P("replica", "fsdp", None),
            P("replica", None),
            P("replica", "fsdp", None),
            P("replica", "fsdp", None),
            P("fsdp", None),
            P("fsdp", None),
            P("replica", "fsdp", None),
        ),
        out_specs=(
            P("replica", "fsdp", None),
            P("fsdp", None),
            P("fsdp", None),
            P("replica", "fsdp", None),
        ),
        check_vma=False,
    )
```

```python
import math

import jax
import jax.numpy as jnp
from jax import lax
from jax.experimental import pallas as pl
from jax.experimental.pallas import tpu as pltpu
from jax.sharding import PartitionSpec as P

CHIPS = 4
CORES = 2
SAME = [[CORES * z + c for z in range(CHIPS)] for c in range(CORES)]
SWAP = [(i, i ^ 1) for i in range(CHIPS * CORES)]
F32 = jnp.float32
BF16 = jnp.bfloat16
GRAD_TILES = 4


def chips_all_to_all(x):
    return lax.all_to_all(
        x, "fsdp", split_axis=0, concat_axis=0, axis_index_groups=SAME, tiled=True
    )


def split_kernel(tok, out, held, come, go):
    wide = out.shape[2]
    ins = [
        pltpu.make_async_copy(tok.at[:, pl.ds(z * wide, wide)], held.at[z], come.at[z])
        for z in range(CHIPS)
    ]
    outs = [pltpu.make_async_copy(held.at[z], out.at[z], go.at[z]) for z in range(CHIPS)]
    for copy in ins:
        copy.start()
    for copy, after in zip(ins, outs):
        copy.wait()
        after.start()
    for after in outs:
        after.wait()


def split_features(tok):
    rows, width = tok.shape
    shape = (CHIPS, rows, width // CHIPS)
    return pl.pallas_call(
        split_kernel,
        out_shape=jax.ShapeDtypeStruct(shape, tok.dtype),
        in_specs=[pl.BlockSpec(memory_space=pl.ANY)],
        out_specs=pl.BlockSpec(memory_space=pl.ANY),
        scratch_shapes=[
            pltpu.VMEM(shape, tok.dtype),
            pltpu.SemaphoreType.DMA((CHIPS,)),
            pltpu.SemaphoreType.DMA((CHIPS,)),
        ],
        cost_estimate=pl.CostEstimate(flops=0, bytes_accessed=4 * rows * width, transcendentals=0),
    )(tok)


def keys_kernel(place, x, mine, other, offset, out):
    chips, rows, wide = x.shape
    depth, cols = mine.shape
    near = x[:, :, pl.ds(pl.multiple_of(place[0] * depth, depth), depth)]
    far = x[:, :, pl.ds(pl.multiple_of((1 - place[0]) * depth, depth), depth)]
    near = near.reshape(chips * rows, depth)
    far = far.reshape(chips * rows, depth)
    for at in range(0, cols, 256):
        part = pl.ds(at, 256)
        total = jnp.dot(near, mine[:, part], preferred_element_type=F32)
        total = total + jnp.dot(far, other[:, part], preferred_element_type=F32)
        for z in range(chips):
            own = (place[1] == z).astype(F32)
            out[z, :, part] = (total[z * rows:(z + 1) * rows] - own * offset[:, part]).astype(out.dtype)


def partial_keys(place, x, mine, other, offset):
    chips, rows, wide = x.shape
    cols = mine.shape[1]
    vmem = pl.BlockSpec(memory_space=pltpu.VMEM)
    return pl.pallas_call(
        keys_kernel,
        in_specs=[pl.BlockSpec(memory_space=pltpu.SMEM), vmem, vmem, vmem, vmem],
        out_specs=vmem,
        out_shape=jax.ShapeDtypeStruct((chips, rows, cols), BF16),
        compiler_params=pltpu.CompilerParams(vmem_limit_bytes=16 << 20),
        cost_estimate=pl.CostEstimate(
            flops=2 * chips * rows * wide * cols,
            bytes_accessed=2 * (chips * rows * (wide + cols) + wide * cols),
            transcendentals=0,
        ),
    )(place, x, mine, other, offset)


def quantize_kernel(base, params, out):
    for k in range(base.shape[1] // 128):
        at = pl.ds(k * 128, 128)
        delta = base[:, at] - params[:, at].astype(F32)
        scale = (jnp.max(jnp.abs(delta), axis=-1, keepdims=True) + 1e-06).astype(BF16).astype(F32)
        quant = (delta * (448.0 / scale)).astype(BF16)
        out[:, at] = (quant.astype(F32) * (scale / 448.0)).astype(BF16)


def quantize(base, params):
    return pl.pallas_call(
        quantize_kernel,
        out_shape=jax.ShapeDtypeStruct(base.shape, BF16),
        cost_estimate=pl.CostEstimate(
            flops=8 * base.size, bytes_accessed=8 * base.size, transcendentals=0
        ),
    )(base, params)


def gradient_kernel(x, a, first, gain, out, theirs, held, come, go):
    depth = x.shape[1]
    tile = depth // GRAD_TILES
    copies = []
    ins = []
    for k in range(GRAD_TILES):
        part = pl.ds(k * tile, tile)
        ins.append(pltpu.make_async_copy(x.at[:, part], theirs.at[:, part], come.at[k]))
        ins[k].start()
    for k in range(GRAD_TILES):
        part = pl.ds(k * tile, tile)
        ins[k].wait()
        total = first[part] + lax.dot_general(
            theirs[:, part], a[...], (((0,), (0,)), ((), ())), preferred_element_type=F32
        )
        held[part] = (total * gain[part]).astype(held.dtype)
        copy = pltpu.make_async_copy(held.at[part], out.at[part], go.at[k])
        copy.start()
        copies.append(copy)
    for copy in copies:
        copy.wait()


def gradient(x, a, first, gain):
    rows, depth = x.shape
    cols = a.shape[1]
    vmem = pl.BlockSpec(memory_space=pltpu.VMEM)
    return pl.pallas_call(
        gradient_kernel,
        in_specs=[pl.BlockSpec(memory_space=pl.ANY)] + [vmem] * 3,
        out_specs=pl.BlockSpec(memory_space=pl.ANY),
        out_shape=jax.ShapeDtypeStruct((depth, cols), BF16),
        scratch_shapes=[
            pltpu.VMEM((rows, depth), BF16),
            pltpu.VMEM((depth, cols), BF16),
            pltpu.SemaphoreType.DMA((GRAD_TILES,)),
            pltpu.SemaphoreType.DMA((GRAD_TILES,)),
        ],
        compiler_params=pltpu.CompilerParams(vmem_limit_bytes=16 << 20),
        cost_estimate=pl.CostEstimate(
            flops=2 * rows * depth * cols,
            bytes_accessed=2 * rows * (depth + cols) + 6 * depth * cols,
            transcendentals=0,
        ),
    )(x, a, first, gain)


def fours_along_x(replicas):
    return [[r for r in range(replicas) if r % 16 == k] for k in range(16)]


def fours_along_y(replicas):
    return [[4 * b + j for j in range(4)] for b in range(replicas // 4)]


def sum_of_sixteen(x):
    replicas = lax.axis_size("replica")
    for groups in (fours_along_x(replicas), fours_along_y(replicas)):
        got = lax.all_gather(x.astype(BF16), "replica", axis=0, axis_index_groups=groups)
        x = jnp.sum(got.astype(F32), axis=0)
    return x


def add_neighbour(x, bit):
    pairs = [(r, r ^ bit) for r in range(lax.axis_size("replica"))]
    return x + lax.ppermute(x.astype(BF16), "replica", pairs).astype(F32)


def shards(tokens, norm_gain, key_weight, key_target, outer_base, outer_momentum, replica_params):
    tok = tokens[0]
    rows, width = tok.shape
    weights = key_weight[0]
    depth, cols = weights.shape
    me = lax.axis_index("fsdp")
    core = me % CORES
    place = jnp.stack([core, me // CORES]).astype(jnp.int32)
    wide = CORES * depth
    root = 1.0 / math.sqrt(rows * CHIPS * CORES)
    dims = (((0,), (0,)), ((), ()))

    pieces, outer_base, norm_gain = lax.optimization_barrier(
        (split_features(tok), outer_base, norm_gain)
    )
    x = chips_all_to_all(pieces)

    gain = lax.dynamic_slice(norm_gain[0], (me * depth,), (depth,)).astype(F32)[:, None]
    mine = (weights.astype(F32) * gain).astype(BF16)
    other = lax.ppermute(mine, "fsdp", SWAP)
    values = tok.astype(F32)
    inv = lax.rsqrt(jnp.mean(values * values, axis=-1, keepdims=True) + 1e-05)

    offset = key_target[0].astype(F32) / inv
    slope = root * inv * inv
    summed = sum_of_sixteen(add_neighbour(quantize(outer_base, replica_params[0]), 4))

    x, summed, slope, offset = lax.optimization_barrier((x, summed, slope, offset))

    part = partial_keys(place, x, mine, other, offset)
    parts = chips_all_to_all(part)
    x = x.reshape(CHIPS * rows, wide)
    x_mine = lax.dynamic_slice(x, (0, core * depth), (CHIPS * rows, depth))
    x_send = lax.dynamic_slice(x, (0, (1 - core) * depth), (CHIPS * rows, depth))
    x_other = lax.ppermute(x_send, "fsdp", SWAP)

    mean_delta = add_neighbour(summed, 8) / lax.axis_size("replica")
    momentum_next = 0.9 * outer_momentum + mean_delta
    base_next = outer_base - 0.7 * (mean_delta + 0.9 * momentum_next)
    params_next = (0.5 * replica_params.astype(F32) + 0.5 * base_next[None]).astype(BF16)

    keys = jnp.sum(parts.astype(F32), axis=0)
    cot = (keys * slope).astype(BF16)
    cots = lax.all_gather(cot, "fsdp", axis=0, axis_index_groups=SAME)
    cots = cots.reshape(CHIPS * rows, cols)
    cots_other = lax.ppermute(cots, "fsdp", SWAP)
    one = lax.dot_general(x_mine, cots, dims, preferred_element_type=F32)
    key_grad = gradient(x_other, cots_other, one, gain)[None]
    return (key_grad, base_next, momentum_next, params_next)


def solution(mesh):
    return jax.shard_map(
        shards,
        mesh=mesh,
        in_specs=(
            P("replica", "fsdp", None),
            P("replica", None),
            P("replica", "fsdp", None),
            P("replica", "fsdp", None),
            P("fsdp", None),
            P("fsdp", None),
            P("replica", "fsdp", None),
        ),
        out_specs=(
            P("replica", "fsdp", None),
            P("fsdp", None),
            P("fsdp", None),
            P("replica", "fsdp", None),
        ),
        check_vma=False,
    )
```

```python
import math

import jax
import jax.numpy as jnp
from jax import lax
from jax.experimental import pallas as pl
from jax.experimental.pallas import tpu as pltpu
from jax.sharding import PartitionSpec as P

CHIPS = 4
CORES = 2
SAME = [[CORES * z + c for z in range(CHIPS)] for c in range(CORES)]
SWAP = [(i, i ^ 1) for i in range(CHIPS * CORES)]
F32 = jnp.float32
BF16 = jnp.bfloat16
GRAD_TILES = 2


def chips_all_to_all(x):
    return lax.all_to_all(
        x, "fsdp", split_axis=0, concat_axis=0, axis_index_groups=SAME, tiled=True
    )


def split_kernel(tok, out, held, come, go):
    wide = out.shape[2]
    ins = [
        pltpu.make_async_copy(tok.at[:, pl.ds(z * wide, wide)], held.at[z], come.at[z])
        for z in range(CHIPS)
    ]
    outs = [pltpu.make_async_copy(held.at[z], out.at[z], go.at[z]) for z in range(CHIPS)]
    for copy in ins:
        copy.start()
    for copy, after in zip(ins, outs):
        copy.wait()
        after.start()
    for after in outs:
        after.wait()


def split_features(tok):
    rows, width = tok.shape
    shape = (CHIPS, rows, width // CHIPS)
    return pl.pallas_call(
        split_kernel,
        out_shape=jax.ShapeDtypeStruct(shape, tok.dtype),
        in_specs=[pl.BlockSpec(memory_space=pl.ANY)],
        out_specs=pl.BlockSpec(memory_space=pl.ANY),
        scratch_shapes=[
            pltpu.VMEM(shape, tok.dtype),
            pltpu.SemaphoreType.DMA((CHIPS,)),
            pltpu.SemaphoreType.DMA((CHIPS,)),
        ],
        cost_estimate=pl.CostEstimate(flops=0, bytes_accessed=4 * rows * width, transcendentals=0),
    )(tok)


def keys_kernel(place, x, mine, other, offset, out):
    chips, rows, wide = x.shape
    depth, cols = mine.shape
    near = x[:, :, pl.ds(pl.multiple_of(place[0] * depth, depth), depth)]
    far = x[:, :, pl.ds(pl.multiple_of((1 - place[0]) * depth, depth), depth)]
    near = near.reshape(chips * rows, depth)
    far = far.reshape(chips * rows, depth)
    for at in range(0, cols, 256):
        part = pl.ds(at, 256)
        total = jnp.dot(near, mine[:, part], preferred_element_type=F32)
        total = total + jnp.dot(far, other[:, part], preferred_element_type=F32)
        for z in range(chips):
            own = (place[1] == z).astype(F32)
            out[z, :, part] = (total[z * rows:(z + 1) * rows] - own * offset[:, part]).astype(out.dtype)


def partial_keys(place, x, mine, other, offset):
    chips, rows, wide = x.shape
    cols = mine.shape[1]
    vmem = pl.BlockSpec(memory_space=pltpu.VMEM)
    return pl.pallas_call(
        keys_kernel,
        in_specs=[pl.BlockSpec(memory_space=pltpu.SMEM), vmem, vmem, vmem, vmem],
        out_specs=vmem,
        out_shape=jax.ShapeDtypeStruct((chips, rows, cols), BF16),
        compiler_params=pltpu.CompilerParams(vmem_limit_bytes=16 << 20),
        cost_estimate=pl.CostEstimate(
            flops=2 * chips * rows * wide * cols,
            bytes_accessed=2 * (chips * rows * (wide + cols) + wide * cols),
            transcendentals=0,
        ),
    )(place, x, mine, other, offset)


def quantize_kernel(base, params, out):
    for k in range(base.shape[1] // 128):
        at = pl.ds(k * 128, 128)
        delta = base[:, at] - params[:, at].astype(F32)
        scale = (jnp.max(jnp.abs(delta), axis=-1, keepdims=True) + 1e-06).astype(BF16).astype(F32)
        quant = (delta * (448.0 / scale)).astype(BF16)
        out[:, at] = (quant.astype(F32) * (scale / 448.0)).astype(BF16)


def quantize(base, params):
    return pl.pallas_call(
        quantize_kernel,
        out_shape=jax.ShapeDtypeStruct(base.shape, BF16),
        cost_estimate=pl.CostEstimate(
            flops=8 * base.size, bytes_accessed=8 * base.size, transcendentals=0
        ),
    )(base, params)


def gradient_kernel(x, a, first, gain, out, held, go):
    depth = x.shape[1]
    tile = depth // GRAD_TILES
    copies = []
    for k in range(GRAD_TILES):
        part = pl.ds(k * tile, tile)
        total = first[part] + lax.dot_general(
            x[:, part], a[...], (((0,), (0,)), ((), ())), preferred_element_type=F32
        )
        held[part] = (total * gain[part]).astype(held.dtype)
        copy = pltpu.make_async_copy(held.at[part], out.at[part], go.at[k])
        copy.start()
        copies.append(copy)
    for copy in copies:
        copy.wait()


def gradient(x, a, first, gain):
    rows, depth = x.shape
    cols = a.shape[1]
    vmem = pl.BlockSpec(memory_space=pltpu.VMEM)
    return pl.pallas_call(
        gradient_kernel,
        in_specs=[vmem] * 4,
        out_specs=pl.BlockSpec(memory_space=pl.ANY),
        out_shape=jax.ShapeDtypeStruct((depth, cols), BF16),
        scratch_shapes=[pltpu.VMEM((depth, cols), BF16), pltpu.SemaphoreType.DMA((GRAD_TILES,))],
        compiler_params=pltpu.CompilerParams(vmem_limit_bytes=16 << 20),
        cost_estimate=pl.CostEstimate(
            flops=2 * rows * depth * cols,
            bytes_accessed=2 * rows * (depth + cols) + 6 * depth * cols,
            transcendentals=0,
        ),
    )(x, a, first, gain)


def fours_along_x(replicas):
    return [[r for r in range(replicas) if r % 16 == k] for k in range(16)]


def fours_along_y(replicas):
    return [[4 * b + j for j in range(4)] for b in range(replicas // 4)]


def sum_of_sixteen(x):
    replicas = lax.axis_size("replica")
    for groups in (fours_along_x(replicas), fours_along_y(replicas)):
        got = lax.all_gather(x.astype(BF16), "replica", axis=0, axis_index_groups=groups)
        x = jnp.sum(got.astype(F32), axis=0)
    return x


def add_neighbour(x, bit):
    pairs = [(r, r ^ bit) for r in range(lax.axis_size("replica"))]
    return x + lax.ppermute(x.astype(BF16), "replica", pairs).astype(F32)


def shards(tokens, norm_gain, key_weight, key_target, outer_base, outer_momentum, replica_params):
    tok = tokens[0]
    rows, width = tok.shape
    weights = key_weight[0]
    depth, cols = weights.shape
    me = lax.axis_index("fsdp")
    core = me % CORES
    place = jnp.stack([core, me // CORES]).astype(jnp.int32)
    wide = CORES * depth
    root = 1.0 / math.sqrt(rows * CHIPS * CORES)
    dims = (((0,), (0,)), ((), ()))

    pieces, outer_base, norm_gain = lax.optimization_barrier(
        (split_features(tok), outer_base, norm_gain)
    )
    x = chips_all_to_all(pieces)

    gain = lax.dynamic_slice(norm_gain[0], (me * depth,), (depth,)).astype(F32)[:, None]
    mine = (weights.astype(F32) * gain).astype(BF16)
    other = lax.ppermute(mine, "fsdp", SWAP)
    values = tok.astype(F32)
    inv = lax.rsqrt(jnp.mean(values * values, axis=-1, keepdims=True) + 1e-05)

    offset = key_target[0].astype(F32) / inv
    slope = root * inv * inv
    summed = sum_of_sixteen(add_neighbour(quantize(outer_base, replica_params[0]), 4))

    x, summed, slope, offset = lax.optimization_barrier((x, summed, slope, offset))

    part = partial_keys(place, x, mine, other, offset)
    parts = chips_all_to_all(part)
    x = x.reshape(CHIPS * rows, wide)
    x_mine = lax.dynamic_slice(x, (0, core * depth), (CHIPS * rows, depth))
    x_send = lax.dynamic_slice(x, (0, (1 - core) * depth), (CHIPS * rows, depth))
    x_other = lax.ppermute(x_send, "fsdp", SWAP)

    mean_delta = add_neighbour(summed, 8) / lax.axis_size("replica")
    momentum_next = 0.9 * outer_momentum + mean_delta
    base_next = outer_base - 0.7 * (mean_delta + 0.9 * momentum_next)
    params_next = (0.5 * replica_params.astype(F32) + 0.5 * base_next[None]).astype(BF16)

    keys = jnp.sum(parts.astype(F32), axis=0)
    cot = (keys * slope).astype(BF16)
    cots = lax.all_gather(cot, "fsdp", axis=0, axis_index_groups=SAME)
    cots = cots.reshape(CHIPS * rows, cols)
    cots_other = lax.ppermute(cots, "fsdp", SWAP)
    one = lax.dot_general(x_mine, cots, dims, preferred_element_type=F32)
    key_grad = gradient(x_other, cots_other, one, gain)[None]
    return (key_grad, base_next, momentum_next, params_next)


def solution(mesh):
    return jax.shard_map(
        shards,
        mesh=mesh,
        in_specs=(
            P("replica", "fsdp", None),
            P("replica", None),
            P("replica", "fsdp", None),
            P("replica", "fsdp", None),
            P("fsdp", None),
            P("fsdp", None),
            P("replica", "fsdp", None),
        ),
        out_specs=(
            P("replica", "fsdp", None),
            P("fsdp", None),
            P("fsdp", None),
            P("replica", "fsdp", None),
        ),
        check_vma=False,
    )
```
